32 devices in a mesh: pass: 2 (over x), rows: 16 (over z, y, core).
Axes of the slice: x: 2, y: 2, z: 4, core: 2. Of those that a mesh axis runs over, the one named last changes fastest.
Arguments:
- layer_in: bfloat16 [16384, 512], P('rows'), may hold values from -6 to 6
- memory: bfloat16 [16384, 512], P('rows'), may hold values from -6 to 6
- targets: int32 [16384], P('rows'), may hold values from 0 to 15999
- segment_ids: int32 [16, 1024], P('rows'), may hold values from 0 to 7, never falling along the last dimension, each value on 1 to 256 neighbouring positions
- memory_segments: int32 [16, 1024], P('rows'), may hold values from 0 to 7, never falling along the last dimension, each value on 1 to 256 neighbouring positions
- row_length: int32 [16], P('rows'), may hold values from 512 to 1024
- group_sizes: int32 [8], replicated, may hold values from 1 to 4, 16 in all
- pass_experts: int32 [2, 8], P('pass'), may hold values from 0 to 3
- norm_gain: float32 [4, 512], replicated, may hold values from 0.5 to 1.5
- norm_bias: float32 [4, 512], replicated, may hold values from -1 to 1
- self_in: bfloat16 [512, 1536], replicated, may hold values from -0.25 to 0.25
- self_out: bfloat16 [512, 512], replicated, may hold values from -1.5 to 1.5
- cross_query: bfloat16 [512, 512], replicated, may hold values from -0.25 to 0.25
- cross_key_value: bfloat16 [512, 1024], replicated, may hold values from -0.25 to 0.25
- cross_out: bfloat16 [512, 512], replicated, may hold values from -1.5 to 1.5
- attention_bias: float32 [6, 512], replicated, may hold values from -1 to 1
- expert_in: bfloat16 [4, 512, 2048], replicated, may hold values from -0.25 to 0.25
- expert_in_bias: float32 [4, 2048], replicated, may hold values from -0.6 to 0.6
- expert_out: bfloat16 [4, 2048, 512], replicated, may hold values from -0.125 to 0.125
- expert_out_bias: float32 [4, 512], replicated, may hold values from -0.6 to 0.6
- embedding: bfloat16 [16000, 512], replicated, may hold values from -0.5 to 0.5
Outputs:
- token_loss: float32 [2, 16384], P('pass', 'rows')
- layer_in_grad: float32 [16384, 512], P('rows')
- memory_grad: float32 [16384, 512], P('rows')
- norm_gain_grad: float32 [4, 512], P(None, 'rows')
- norm_bias_grad: float32 [4, 512], P(None, 'rows')
- self_in_grad: float32 [512, 1536], P('rows')
- self_out_grad: float32 [512, 512], P('rows')
- cross_query_grad: float32 [512, 512], P('rows')
- cross_key_value_grad: float32 [512, 1024], P('rows')
- cross_out_grad: float32 [512, 512], P('rows')
- attention_bias_grad: float32 [6, 512], P(None, 'rows')
- expert_in_grad: float32 [4, 512, 2048], P(None, 'rows')
- expert_in_bias_grad: float32 [4, 2048], P(None, 'rows')
- expert_out_grad: float32 [4, 2048, 512], P(None, 'rows')
- expert_out_bias_grad: float32 [4, 512], P(None, 'rows')
- embedding_grad: float32 [16000, 512], P('rows')
The draws below stay inside these ranges and needn't reach their ends.
Inputs may be any that keep to these rules, and one draw needn't show every extreme that they name: `segment_ids`: never falls along a row; every number of 0 to 7 occurs in each row. `memory_segments`: never falls along a row; every number of 0 to 7 occurs in each row; number j is the source of the row's document j. Rows are grouped by language pair in order: rows 0 to group_sizes[0] - 1 belong to pair 0, the next group_sizes[1] to pair 1, and so on; the sizes sum to 16.
All inputs are finite; a program needn't handle non-finite values.
Results may differ from the reference program's by a relative error of at most 0.017.
Values may be sent and summed in bfloat16 or wider, within the bound.
No kernel may reach another device: no remote copies, remote signals or barrier semaphores. Data moves between devices by JAX's collectives and lax.ppermute only.
A program may use at most 448 MiB of HBM per device.

```python
import math
import jax
import jax.numpy as jnp
import numpy as np
from jax import lax

D = 512
HEAD_DIM = 64
FF = 2048
VOCAB = 16000
EXPERTS = 4
PAIRS = 8
SEGS = 8
LEN = 1024
MEM = 1024
ROWS = 16
TOKENS = 16384
MEM_TOKENS = 16384


def with_ends(entries, stream_key, least, high):
    longest = entries.shape.index(max(entries.shape))
    spots = []
    for shift in (0, 1):
        where = [jax.random.randint(jax.random.fold_in(stream_key, axis), (), 0, length) for axis, length in enumerate(entries.shape)]
        where[longest] = (where[longest] + shift) % entries.shape[longest]
        spots.append(tuple(where))
    return entries.at[spots[0]].set(least).at[spots[1]].set(high)


def block_scale(rng, dims, cuts, least, top_value):
    def one(dim, blocks):
        draws = jax.random.uniform(jax.random.fold_in(jax.random.fold_in(rng, 6), dim), (blocks,), jnp.float32, least / len(cuts), top_value / len(cuts))
        return jnp.repeat(jnp.exp(draws), dims[dim] // blocks).reshape((-1,) + (1,) * (len(dims) - dim - 1))

    factor_of = one(*cuts[0])
    for cut in cuts[1:]:
        factor_of = factor_of * one(*cut)
    return factor_of


def rank_table(count, skew):
    portions = [(1 << 20) // math.isqrt(rank ** skew) + 1 for rank in range(1, count + 1)]
    deviation = 1 + sum(portions) // (1 << 30)
    return np.cumsum(np.array([max(1, weight // deviation) for weight in portions]))


def ranked(key, extent, amount, lean):
    listing = rank_table(amount, lean)
    lot = jax.random.randint(jax.random.fold_in(key, 1), extent, 0, int(listing[amount - 1]))
    standing = jnp.searchsorted(jnp.asarray(listing, jnp.int32), lot, side="right")
    return jax.random.permutation(jax.random.fold_in(key, 2), amount)[standing].astype(jnp.int32)


def profile(amount, total, reach, lean):
    weights = [(1 << 20) // math.isqrt(grade ** lean) + 1 for grade in range(2, amount + 1)]
    spare, counts = total - reach - (amount - 1), [1] * (amount - 1)
    while spare > 0:
        candidates = [i for i in range(amount - 1) if counts[i] < reach]
        mass, left = sum([weights[i] for i in candidates]), spare
        for i in candidates:
            addition = min(reach - counts[i], max(1, left * weights[i] // mass), spare)
            counts[i] = counts[i] + addition
            spare = spare - addition
    return np.array([reach] + counts)


def uneven_parts(own_key, amount, total, limit, skew):
    if amount == 2:
        one = jax.random.randint(own_key, (), max(1, total - limit), min(limit, total - 1) + 1)
        return jnp.stack([one, total - one])
    tallies = jnp.asarray(profile(amount, total, limit, skew), jnp.int32)
    twos = (amount - 1) // 2
    source_of, taker = tallies[1:1 + 2 * twos:2], tallies[2:2 + 2 * twos:2]
    room = jnp.minimum(source_of - 1, limit - taker)
    passed = jax.random.randint(jax.random.fold_in(own_key, 1), (twos,), 0, 1 << 20) % (room + 1)
    tallies = tallies.at[1:1 + 2 * twos:2].set(source_of - passed).at[2:2 + 2 * twos:2].set(taker + passed)
    return tallies[jax.random.permutation(jax.random.fold_in(own_key, 2), amount)]


def gaussian(own_key, dims, scale, reach, pieces=(), held_as=jnp.bfloat16):
    entries = jax.random.normal(own_key, dims, jnp.float32) * scale
    if len(pieces) > 0:
        entries = block_scale(own_key, dims, pieces, -0.22, 0.18) * entries
    return jnp.clip(entries, min=-reach, max=reach).astype(held_as)


def setup_inputs(seed: int = 0) -> dict:
    keys = jax.random.split(jax.random.key(seed), 22)
    return {
        "layer_in": gaussian(keys[0], (TOKENS, D), 1.0, 6.0, ((0, 16),)),
        "memory": gaussian(keys[1], (MEM_TOKENS, D), 1.0, 6.0, ((0, 16),)),
        "targets": with_ends(ranked(keys[2], (TOKENS,), VOCAB, 2), jax.random.fold_in(keys[2], 3), 0, VOCAB - 1).astype(jnp.int32),
        "segment_ids": jax.vmap(lambda own: jnp.searchsorted(jnp.cumsum(uneven_parts(own, SEGS, LEN, LEN // 4, 1)), jnp.arange(LEN), side="right"))(jax.random.split(keys[3], ROWS)).reshape((ROWS, LEN)).astype(jnp.int32),
        "memory_segments": jax.vmap(lambda own: jnp.searchsorted(jnp.cumsum(uneven_parts(own, SEGS, MEM, MEM // 4, 1)), jnp.arange(MEM), side="right"))(jax.random.split(keys[4], ROWS)).reshape((ROWS, MEM)).astype(jnp.int32),
        "row_length": with_ends(jax.random.randint(keys[5], (ROWS,), LEN // 2, LEN + 1), jax.random.fold_in(keys[5], 1), LEN // 2, LEN).astype(jnp.int32),
        "group_sizes": uneven_parts(keys[6], PAIRS, ROWS, ROWS // 4, 2).astype(jnp.int32),
        "pass_experts": with_ends(jax.random.randint(keys[7], (2, PAIRS), 0, EXPERTS), jax.random.fold_in(keys[7], 1), 0, EXPERTS - 1).astype(jnp.int32),
        "norm_gain": jnp.clip(1.0 + 0.1 * jax.random.normal(keys[8], (4, D), jnp.float32), 0.5, 1.5),
        "norm_bias": gaussian(keys[9], (4, D), 0.2, 1.0, (), jnp.float32),
        "self_in": gaussian(keys[10], (D, 3 * D), D ** -0.5, 0.25),
        "self_out": gaussian(keys[11], (D, D), (D // 32) ** -0.5, 1.5),
        "cross_query": gaussian(keys[12], (D, D), D ** -0.5, 0.25),
        "cross_key_value": gaussian(keys[13], (D, 2 * D), D ** -0.5, 0.25),
        "cross_out": gaussian(keys[14], (D, D), (D // 32) ** -0.5, 1.5),
        "attention_bias": gaussian(keys[15], (6, D), 0.2, 1.0, (), jnp.float32),
        "expert_in": gaussian(keys[16], (EXPERTS, D, FF), D ** -0.5, 0.25),
        "expert_in_bias": gaussian(keys[17], (EXPERTS, FF), 0.1, 0.6, (), jnp.float32),
        "expert_out": gaussian(keys[18], (EXPERTS, FF, D), FF ** -0.5, 0.125),
        "expert_out_bias": gaussian(keys[19], (EXPERTS, D), 0.1, 0.6, (), jnp.float32),
        "embedding": gaussian(keys[20], (VOCAB, D), (D // 4) ** -0.5, 0.5),
    }


@jax.custom_vjp
def low(v):
    return lax.optimization_barrier(v.astype(jnp.bfloat16)).astype(jnp.float32)

@jax.custom_vjp
def low_back(v):
    return v

def low_keep(v):
    return (low(v), None)

def low_pass(kept, grad):
    return (grad,)

def back_keep(v):
    return (v, None)

def back_low(kept, grad):
    return (low(grad),)
low.defvjp(low_keep, low_pass)
low_back.defvjp(back_keep, back_low)
NORM_EPS = 1e-05
SMOOTHING = 0.1
KL_WEIGHT = 5.0
MASKED = -1e+30
HIGHEST = lax.Precision.HIGHEST

def layer_norm(values, norm_scale, norm_shift):
    row_mean = lax.optimization_barrier(jnp.mean(values, axis=-1, keepdims=True))
    centred = values - row_mean
    spread = lax.optimization_barrier(jnp.mean(centred * centred, axis=-1, keepdims=True))
    return centred * lax.rsqrt(spread + NORM_EPS) * norm_scale + norm_shift

def product(left, right):
    return jnp.dot(low(left), right, precision=HIGHEST, preferred_element_type=jnp.float32)

def attend(query_rows, key_rows, value_rows, allowed):
    head_count = query_rows.shape[1] // HEAD_DIM
    query_heads = query_rows.reshape(query_rows.shape[0], head_count, HEAD_DIM)
    key_heads = key_rows.reshape(key_rows.shape[0], head_count, HEAD_DIM)
    value_heads = value_rows.reshape(value_rows.shape[0], head_count, HEAD_DIM)
    raw_scores = low_back(jnp.einsum('qhd,khd->hqk', query_heads, key_heads, precision=HIGHEST))
    scores = jnp.where(allowed[None], raw_scores * HEAD_DIM ** (-0.5), MASKED)
    row_peak = lax.optimization_barrier(jnp.max(scores, axis=-1, keepdims=True))
    exponent = jnp.exp(scores - row_peak)
    attn_weights = exponent / lax.optimization_barrier(jnp.sum(exponent, axis=-1, keepdims=True))
    mixture = low_back(jnp.einsum('hqk,khd->qhd', low(attn_weights), value_heads, precision=HIGHEST))
    return mixture.reshape(query_rows.shape[0], head_count * HEAD_DIM)

def one_pass(params, input_row, memory_row, expert, self_allowed, cross_allowed):
    norm_scales, norm_shifts, w_self_in, w_self_out, w_cross_query, w_cross_kv, w_cross_out, biases, w_expert_in, b_expert_in, w_expert_out, b_expert_out, w_embed = params
    zero_row = jnp.zeros((D,), jnp.float32)
    normed = layer_norm(input_row, norm_scales[0], norm_shifts[0])
    packed = low(low_back(product(normed, w_self_in) + jnp.concatenate([biases[0], zero_row, biases[1]])))
    mixture = attend(packed[:, :D], packed[:, D:2 * D], packed[:, 2 * D:], self_allowed)
    after_self = input_row + low_back(product(mixture, w_self_out) + biases[2])
    normed = layer_norm(after_self, norm_scales[1], norm_shifts[1])
    queries = low(low_back(product(normed, w_cross_query) + biases[3]))
    key_value = low(low_back(product(memory_row, w_cross_kv) + jnp.concatenate([zero_row, biases[4]])))
    mixture = attend(queries, key_value[:, :D], key_value[:, D:], cross_allowed)
    after_cross = after_self + low_back(product(mixture, w_cross_out) + biases[5])
    normed = layer_norm(after_cross, norm_scales[2], norm_shifts[2])
    expert_pre = low_back(product(normed, w_expert_in[expert]) + b_expert_in[expert])
    activation = jax.nn.gelu(expert_pre, approximate=False)
    after_ffn = after_cross + low_back(product(activation, w_expert_out[expert]) + b_expert_out[expert])
    final_norm = layer_norm(after_ffn, norm_scales[3], norm_shifts[3])
    logits = low_back(product(final_norm, w_embed.T))
    row_peak = lax.optimization_barrier(jnp.max(logits, axis=-1, keepdims=True))
    return logits - row_peak - jnp.log(lax.optimization_barrier(jnp.sum(jnp.exp(logits - row_peak), axis=-1, keepdims=True)))

def smoothed(log_probs, target):
    picked = jnp.take_along_axis(log_probs, target[:, None], axis=1)[:, 0]
    return -(1.0 - SMOOTHING) * picked - SMOOTHING / VOCAB * lax.optimization_barrier(jnp.sum(log_probs, axis=-1))

def row_loss(params, row_item):
    input_row, memory_row, target, segment, memory_segment, row_len, expert_pair = row_item
    position = jnp.arange(LEN, dtype=jnp.int32)
    self_allowed = (segment[:, None] == segment[None, :]) & (position[None, :] <= position[:, None])
    cross_allowed = segment[:, None] == memory_segment[None, :]
    first_pass = one_pass(params, input_row, memory_row, expert_pair[0], self_allowed, cross_allowed)
    second_pass = one_pass(params, input_row, memory_row, expert_pair[1], self_allowed, cross_allowed)
    low_first = low(first_pass)
    low_second = low(second_pass)
    divergence = lax.optimization_barrier(jnp.sum((jnp.exp(low_first) - jnp.exp(low_second)) * (low_first - low_second), axis=-1))
    counted = (position < row_len).astype(jnp.float32)
    loss_first = counted * (smoothed(first_pass, target) + 0.5 * KL_WEIGHT * divergence)
    loss_second = counted * (smoothed(second_pass, target) + 0.5 * KL_WEIGHT * divergence)
    return (jnp.sum(loss_first) + jnp.sum(loss_second), (loss_first, loss_second))

def reference(layer_in, memory, targets, segment_ids, memory_segments, row_length, group_sizes, pass_experts, norm_gain, norm_bias, self_in, self_out, cross_query, cross_key_value, cross_out, attention_bias, expert_in, expert_in_bias, expert_out, expert_out_bias, embedding):
    bounds = jnp.cumsum(group_sizes)
    row_ids = jnp.arange(ROWS, dtype=jnp.int32)
    pair_of_row = lax.optimization_barrier(jnp.sum((bounds[None, :] <= row_ids[:, None]).astype(jnp.int32), axis=1))
    expert_pairs = jnp.transpose(pass_experts[:, pair_of_row])
    params = tuple((weight.astype(jnp.float32) for weight in (norm_gain, norm_bias, self_in, self_out, cross_query, cross_key_value, cross_out, attention_bias, expert_in, expert_in_bias, expert_out, expert_out_bias, embedding)))
    input_rows = layer_in.astype(jnp.float32).reshape(ROWS, LEN, D)
    memory_rows = memory.astype(jnp.float32).reshape(ROWS, MEM, D)
    target_rows = targets.reshape(ROWS, LEN)

    def summed_loss(params, input_rows, memory_rows):

        def per_row(row_item):
            return row_loss(params, row_item)
        row_sums, losses = lax.map(jax.checkpoint(per_row), (input_rows, memory_rows, target_rows, segment_ids, memory_segments, row_length, expert_pairs))
        return (jnp.sum(row_sums), losses)
    loss_sum, pullback, losses = jax.vjp(summed_loss, params, input_rows, memory_rows, has_aux=True)
    grad_params, grad_input, grad_memory = pullback(jnp.ones_like(loss_sum))
    g_gain, g_bias, g_self_in, g_self_out, g_cross_query, g_cross_kv, g_cross_out, g_attn_bias, g_expert_in, g_expert_in_bias, g_expert_out, g_expert_out_bias, g_embedding = grad_params
    token_loss = jnp.stack([losses[0].reshape(-1), losses[1].reshape(-1)])
    return (token_loss, grad_input.reshape(TOKENS, D), grad_memory.reshape(MEM_TOKENS, D), g_gain, g_bias, g_self_in, g_self_out, g_cross_query, g_cross_kv, g_cross_out, g_attn_bias, g_expert_in, g_expert_in_bias, g_expert_out, g_expert_out_bias, g_embedding)
```

```python
import functools
import math

import jax
import jax.numpy as jnp
from jax import lax
from jax.experimental import pallas as pl
from jax.experimental.pallas import tpu as pltpu
from jax.sharding import PartitionSpec as P

HEAD_DIM = 64
SPAN = 256
LANES = 128

NORM_EPS = 1e-05
SMOOTHING = 0.1
KL_WEIGHT = 5.0
MASKED = -1e30
F32 = jnp.float32
BF16 = jnp.bfloat16
NT = (((1,), (1,)), ((), ()))
TN = (((0,), (0,)), ((), ()))


def dot(left, right, dims=(((1,), (0,)), ((), ()))):
    return lax.dot_general(left, right, dims, preferred_element_type=F32)


def kernel_params(mib):
    return pltpu.CompilerParams(vmem_limit_bytes=mib * 2**20)


def kernel_cost(products, moved, exps):
    return pl.CostEstimate(flops=2 * products, bytes_accessed=moved, transcendentals=exps)


def norm_parts(values):
    row_mean = jnp.mean(values, axis=-1, keepdims=True)
    centred = values - row_mean
    spread = jnp.mean(centred * centred, axis=-1, keepdims=True)
    inverse = lax.rsqrt(spread + NORM_EPS)
    return centred * inverse, inverse


def norm_apply(values, gain, bias):
    unit, unused = norm_parts(values)
    return unit * gain + bias


def norm_backward(values, gain, grad_normed):
    unit, inverse = norm_parts(values)
    scaled = grad_normed * gain
    first = jnp.mean(scaled, axis=-1, keepdims=True)
    second = jnp.mean(scaled * unit, axis=-1, keepdims=True)
    grad = inverse * (scaled - first - unit * second)
    return (
        grad,
        jnp.sum(grad_normed * unit, axis=0, keepdims=True),
        jnp.sum(grad_normed, axis=0, keepdims=True),
    )


def row_sums(values):
    return jnp.sum(values.astype(F32), axis=0, keepdims=True)


def as_column(row):
    return jnp.broadcast_to(row.astype(F32), (8, row.shape[1])).T[:, 0:1]


def own_half(ref, side, count, block):
    return ref[pl.ds(pl.multiple_of(side * count, block), count), :]


def store_halves(ref, index, values, side):
    half = values.shape[-1] // 2
    first, second = values[:, :half], values[:, half:]
    ref[index + (0,)] = jnp.where(side == 0, first, second).astype(ref.dtype)
    ref[index + (1,)] = jnp.where(side == 0, second, first).astype(ref.dtype)


def staged_terms(keep_ref, send_ref, number, left, right, order_ref, side):
    ordered = dot(left, order_ref[...]).astype(BF16)
    term = dot(ordered, right, TN)
    middle = term.shape[0] // 2
    store_halves(keep_ref, (number,), term[:middle], side)
    store_halves(send_ref, (number,), term[middle:], side)


def without(kernel, start, count):
    return lambda *refs: kernel(*refs[:start], *refs[start + count :])


ANY = pl.BlockSpec(memory_space=pl.ANY)
VMEM = pl.BlockSpec(memory_space=pltpu.VMEM)
SMEM = pl.BlockSpec(memory_space=pltpu.SMEM)


def head_lanes(block, head):
    lane = lax.broadcasted_iota(jnp.int32, block.shape, 1)
    keep = (lane < HEAD_DIM) if head == 0 else (lane >= HEAD_DIM)
    return jnp.where(keep, block, jnp.zeros_like(block))


def allowed_keys(seg_query, seg_key, span, causal):
    q0, qn, k0, kn = span
    allowed = seg_key[k0 : k0 + kn, :] == seg_query[:, q0 : q0 + qn]
    if causal:
        key_place = lax.broadcasted_iota(jnp.int32, (kn, qn), 0) + (k0 - SPAN)
        query_place = lax.broadcasted_iota(jnp.int32, (kn, qn), 1) + q0
        allowed = allowed & (key_place <= query_place)
    return allowed


def pair_columns(base, pair):
    return pl.ds(pl.multiple_of(base + pair * LANES, LANES), LANES)


def attend_forward(q_ref, k_ref, v_ref, bases, q_shift, seg_query, seg_key, spans, causal, mix_ref, lse_ref):
    scale = HEAD_DIM ** (-0.5)
    q_base, k_base, v_base = bases

    def one_pair(pair, carry):
        for span in spans:
            q0, qn, k0, kn = span
            query = q_ref[q_shift + q0 : q_shift + q0 + qn, pair_columns(q_base, pair)]
            query = (query.astype(F32) * scale).astype(BF16)
            key = k_ref[k0 : k0 + kn, pair_columns(k_base, pair)]
            value_t = v_ref[k0 : k0 + kn, pair_columns(v_base, pair)].T
            allowed = allowed_keys(seg_query, seg_key, span, causal)
            mixed = []
            for head in range(2):
                scores = jnp.where(allowed, dot(head_lanes(key, head), query, NT), MASKED)
                peak = jnp.max(scores, axis=0, keepdims=True)
                exponent = jnp.exp(scores - peak)
                total = jnp.sum(exponent, axis=0, keepdims=True)
                part = dot(
                    value_t[head * HEAD_DIM : (head + 1) * HEAD_DIM, :], exponent.astype(BF16)
                )
                mixed.append(part * (1.0 / total))
                lse_ref[pair, head : head + 1, q0 : q0 + qn] = peak + jnp.log(total)
            mix_ref[q0 : q0 + qn, pair_columns(0, pair)] = (
                jnp.concatenate(mixed, axis=0).T.astype(BF16)
            )
        return carry

    lax.fori_loop(0, mix_ref.shape[1] // LANES, one_pair, 0)


def attend_backward(
    q_ref, k_ref, v_ref, bases, q_shift, g_ref, seg_query, seg_key, lse_ref, spans, causal,
    dq_ref, dk_ref, dv_ref,
):
    scale = HEAD_DIM ** (-0.5)
    q_base, k_base, v_base = bases

    def one_pair(pair, carry):
        own = pair_columns(0, pair)
        dk_ref[:, own] = jnp.zeros((dk_ref.shape[0], LANES), F32)
        dv_ref[:, own] = jnp.zeros((dv_ref.shape[0], LANES), F32)
        for span in spans:
            q0, qn, k0, kn = span
            query = q_ref[q_shift + q0 : q_shift + q0 + qn, pair_columns(q_base, pair)]
            query = (query.astype(F32) * scale).astype(BF16)
            key = k_ref[k0 : k0 + kn, pair_columns(k_base, pair)]
            value = v_ref[k0 : k0 + kn, pair_columns(v_base, pair)]
            grad = g_ref[q0 : q0 + qn, own]
            key_t = key.T
            allowed = allowed_keys(seg_query, seg_key, span, causal)
            grad_queries = []
            for head in range(2):
                scores = jnp.where(allowed, dot(head_lanes(key, head), query, NT), MASKED)
                weights = jnp.exp(scores - lse_ref[pair, head : head + 1, q0 : q0 + qn])
                grad_weights = dot(head_lanes(value, head), grad, NT)
                weighted = jnp.sum(weights * grad_weights, axis=0, keepdims=True)
                grad_raw = (weights * (grad_weights - weighted)).astype(BF16)
                grad_queries.append(
                    dot(key_t[head * HEAD_DIM : (head + 1) * HEAD_DIM, :], grad_raw) * scale
                )
                dk_ref[k0 : k0 + kn, own] += dot(grad_raw, head_lanes(query, head))
                dv_ref[k0 : k0 + kn, own] += dot(weights.astype(BF16), head_lanes(grad, head))
            dq_ref[q0 : q0 + qn, own] = jnp.concatenate(grad_queries, axis=0).T.astype(BF16)
        return carry

    lax.fori_loop(0, dq_ref.shape[1] // LANES, one_pair, 0)


def self_segments(side, seg_ref, half):
    own = seg_ref[:, pl.ds(pl.multiple_of(side * half, SPAN), half)]
    halo = seg_ref[:, pl.ds(pl.multiple_of(side * (half - SPAN), SPAN), SPAN)]
    halo = jnp.where(side == 1, halo, -1)
    return own.astype(F32), as_column(jnp.concatenate([halo, own], axis=1))


def span_lists(half, mem_length):
    blocks = range(0, half, SPAN)
    return [(q0, SPAN, q0, 2 * SPAN) for q0 in blocks], [(q0, SPAN, 0, mem_length) for q0 in blocks]


def layer_forward_kernel(
    side_ref, x_ref, mem_ref, seg_ref, mseg_ref, gain_ref, shift_ref, si_ref, so_ref, cq_ref, ckv_ref,
    co_ref, ab_ref,
    ns_ref, qkv_ref, self_mix_ref, self_lse_ref, after_self_ref, nc_ref, queries_ref, kv_ref,
    cross_mix_ref, cross_lse_ref, after_cross_ref, nf_ref,
):
    side = side_ref[0]
    half, width = after_self_ref.shape
    halo = x_ref[pl.ds(pl.multiple_of(side * (half - SPAN), SPAN), SPAN), :].astype(F32)
    own = own_half(x_ref, side, half, SPAN).astype(F32)
    self_spans, cross_spans = span_lists(half, mem_ref.shape[0])
    normed = norm_apply(jnp.concatenate([halo, own], axis=0), gain_ref[0:1], shift_ref[0:1])
    normed = normed.astype(BF16)
    ns_ref[...] = normed[SPAN:]
    for third, bias in enumerate((ab_ref[0:1], 0.0, ab_ref[1:2])):
        cols = slice(third * width, (third + 1) * width)
        qkv_ref[:, cols] = (dot(normed, si_ref[:, cols]) + bias).astype(BF16)
    seg_query, seg_key = self_segments(side, seg_ref, half)
    attend_forward(
        qkv_ref, qkv_ref, qkv_ref, (0, width, 2 * width), SPAN, seg_query, seg_key, self_spans, True,
        self_mix_ref, self_lse_ref,
    )
    for half_kv, bias in enumerate((0.0, ab_ref[4:5])):
        cols = slice(half_kv * width, (half_kv + 1) * width)
        kv_ref[:, cols] = (dot(mem_ref[...], ckv_ref[:, cols]) + bias).astype(BF16)
    after_self = own + dot(self_mix_ref[...], so_ref[...]) + ab_ref[2:3]
    after_self_ref[...] = after_self
    normed = norm_apply(after_self, gain_ref[1:2], shift_ref[1:2]).astype(BF16)
    nc_ref[...] = normed
    queries_ref[...] = (dot(normed, cq_ref[...]) + ab_ref[3:4]).astype(BF16)
    attend_forward(
        queries_ref, kv_ref, kv_ref, (0, 0, width), 0, seg_query, as_column(mseg_ref[...]),
        cross_spans, False, cross_mix_ref, cross_lse_ref,
    )
    after_cross = after_self + dot(cross_mix_ref[...], co_ref[...]) + ab_ref[5:6]
    after_cross_ref[...] = after_cross
    nf_ref[...] = norm_apply(after_cross, gain_ref[2:3], shift_ref[2:3]).astype(BF16)


def layer_forward(side, layer_in, memory, segment, mem_segment, gain, shift, weights, biases):
    length, width = layer_in.shape
    half = length // 2
    mem_length = memory.shape[0]
    pairs = width // LANES
    out = lambda shape, dtype: jax.ShapeDtypeStruct(shape, dtype)
    return pl.pallas_call(
        layer_forward_kernel,
        in_specs=[SMEM] + [VMEM] * 12,
        out_specs=[VMEM] * 12,
        out_shape=[
            out((half, width), BF16),
            out((half + SPAN, 3 * width), BF16),
            out((half, width), BF16),
            out((pairs, 2, half), F32),
            out((half, width), F32),
            out((half, width), BF16),
            out((half, width), BF16),
            out((mem_length, 2 * width), BF16),
            out((half, width), BF16),
            out((pairs, 2, half), F32),
            out((half, width), F32),
            out((half, width), BF16),
        ],
        compiler_params=kernel_params(56),
        cost_estimate=kernel_cost(30 * half * width * width, 2**24, half * mem_length * 16),
    )(side, layer_in, memory, segment, mem_segment, gain, shift, *weights, biases)


def expert_names_kernel(sizes_ref, own_ref, other_ref, place_ref, side_ref, names_ref, first_ref, second_ref):
    side = side_ref[0]
    for number in range(2):
        row = place_ref[0] ^ number
        pair = jnp.int32(0)
        bound = jnp.int32(0)
        for index in range(sizes_ref.shape[0] - 1):
            bound = bound + sizes_ref[index]
            pair = pair + (bound <= row).astype(jnp.int32)
        own, other = own_ref[0, pair], other_ref[0, pair]
        names_ref[2 * number] = jnp.where(side == 0, own, other)
        names_ref[2 * number + 1] = jnp.where(side == 0, other, own)
    for number, ref in enumerate((first_ref, second_ref)):
        ref[0] = names_ref[number]
        ref[1] = place_ref[0]
        ref[2] = side


def expert_names(sizes, own, other, place, side):
    words = lambda count: jax.ShapeDtypeStruct((count,), jnp.int32)
    return pl.pallas_call(
        expert_names_kernel,
        in_specs=[SMEM] * 5,
        out_specs=[SMEM] * 3,
        out_shape=[words(4), words(3), words(3)],
    )(sizes, own, other, place, side)


def experts_forward_kernel(
    names, nf_ref, after_ref, wi_ref, bi_ref, wo_ref, bo_ref, gain_ref, shift_ref,
    act_ref, slope_ref, final_ref, after_ffn_ref, total,
):
    chunk = pl.program_id(1)
    pre = dot(nf_ref[...], wi_ref[0]) + bi_ref[0]
    phi = 0.5 * (1.0 + lax.erf(pre * math.sqrt(0.5)))
    bell = jnp.exp(-0.5 * pre * pre) * (1.0 / math.sqrt(2.0 * math.pi))
    act = (pre * phi).astype(BF16)
    act_ref[0] = act
    slope_ref[0] = (phi + pre * bell).astype(BF16)

    @pl.when(chunk == 0)
    def start():
        total[...] = after_ref[...] + bo_ref[0]

    total[...] += dot(act, wo_ref[0])

    @pl.when(chunk == pl.num_programs(1) - 1)
    def finish():
        after_ffn_ref[0] = total[...]
        final_ref[...] = norm_apply(total[...], gain_ref[3:4], shift_ref[3:4]).astype(BF16)


FF_CHUNKS = 4
EXPERT_ROWS = 8


def experts_forward(names, normed, after_cross, w_in, b_in, w_out, b_out, gain, shift):
    tokens, width = normed.shape
    experts, unused, hidden = w_in.shape
    block = hidden // FF_CHUNKS
    whole = lambda shape: pl.BlockSpec(shape, lambda p, c, names: (0, 0))
    return pl.pallas_call(
        experts_forward_kernel,
        grid_spec=pltpu.PrefetchScalarGridSpec(
            num_scalar_prefetch=1,
            grid=(2, FF_CHUNKS),
            in_specs=[
                whole((tokens, width)),
                whole((tokens, width)),
                pl.BlockSpec((1, width, block), lambda p, c, names: (names[p], 0, c)),
                pl.BlockSpec((1, 1, block), lambda p, c, names: (names[p], 0, c)),
                pl.BlockSpec((1, block, width), lambda p, c, names: (names[p], c, 0)),
                pl.BlockSpec((1, 1, width), lambda p, c, names: (names[p], 0, 0)),
                whole((4, width)),
                whole((4, width)),
            ],
            out_specs=[
                pl.BlockSpec((1, tokens, block), lambda p, c, names: (p, 0, c)),
                pl.BlockSpec((1, tokens, block), lambda p, c, names: (p, 0, c)),
                pl.BlockSpec((tokens, width), lambda p, c, names: (p, 0)),
                pl.BlockSpec((1, tokens, width), lambda p, c, names: (p, 0, 0)),
            ],
            scratch_shapes=[pltpu.VMEM((tokens, width), F32)],
        ),
        out_shape=[
            jax.ShapeDtypeStruct((2, tokens, hidden), BF16),
            jax.ShapeDtypeStruct((2, tokens, hidden), BF16),
            jax.ShapeDtypeStruct((2 * tokens, width), BF16),
            jax.ShapeDtypeStruct((2, tokens, width), F32),
        ],
        compiler_params=kernel_params(40),
        cost_estimate=kernel_cost(4 * tokens * width * hidden, 2**24, 4 * tokens * hidden),
    )(
        names, normed, after_cross, w_in, b_in.reshape(experts, 1, hidden), w_out,
        b_out.reshape(experts, 1, width), gain, shift,
    )


def experts_backward_kernel(
    number, plain, scalars, gf_ref, after_ffn_ref, act_ref, slope_ref, wi_ref, wo_ref, order_ref,
    gain_ref, *refs
):
    if number == 1:
        old_bias_ref, old_grad_ref, old_nf_ref, old_vec_ref, after_cross_ref, co_ref, *refs = refs
        (ik_ref, is_ref, ok_ref, os_ref, bias_ref, vec_ref, gc_ref, gco_ref, gcm_ref,
         gffn, gnf) = refs
    else:
        ik_ref, is_ref, ok_ref, os_ref, bias_ref, vec_ref, gc_ref, gnf, gffn = refs
    chunk = pl.program_id(0)
    place, side = scalars[1], scalars[2]

    @pl.when(chunk == 0)
    def start():
        grad, gain_part, shift_part = norm_backward(
            after_ffn_ref[0], gain_ref[3:4], gf_ref[...]
        )
        gffn[...] = grad.astype(BF16)
        vec_ref[...] = jnp.zeros_like(vec_ref) if number == 0 else old_vec_ref[...]
        vec_ref[0:1] += gain_part
        vec_ref[1:2] += shift_part
        experts_here = lax.broadcasted_iota(jnp.int32, (EXPERT_ROWS, 1), 0) == scalars[0]
        vec_ref[8:] += jnp.where(experts_here, row_sums(gffn[...]), 0.0)
        if number == 0:
            gc_ref[...] = grad
            gnf[...] = jnp.zeros_like(gnf)
        else:
            gc_ref[...] = old_grad_ref[...] + grad
            gnf[...] = old_nf_ref[...]

    grad_out = gffn[...]
    grad_act = dot(grad_out, wo_ref[0], NT)
    grad_pre = (grad_act * slope_ref[0].astype(F32)).astype(BF16)
    experts_here = lax.broadcasted_iota(jnp.int32, (EXPERT_ROWS, 1), 0) == scalars[0]
    biases = jnp.where(experts_here, row_sums(grad_pre), 0.0)
    bias_ref[...] = biases if number == 0 else old_bias_ref[...] + biases
    gnf[...] += dot(grad_pre, wi_ref[0], NT)
    term_in = dot(order_ref[...], grad_pre, TN)
    middle = term_in.shape[0] // 2
    store_halves(ik_ref, (0,), term_in[:middle], side)
    store_halves(is_ref, (0,), term_in[middle:], side)
    term_out = dot(act_ref[0], grad_out, TN)
    if plain:
        store_halves(ok_ref, (), term_out, side)
    else:
        size = ok_ref.shape[2]
        lanes = ok_ref.shape[3]
        here = term_out.shape[0] // size
        for pair in range(here // 2):
            first = term_out[2 * pair * size : (2 * pair + 1) * size]
            second = term_out[(2 * pair + 1) * size : (2 * pair + 2) * size]
            even = lax.rem(place, 2) == 0
            target = lax.shift_right_logical(place ^ (chunk * here + 2 * pair), 1)
            for ref, part in ((ok_ref, jnp.where(even, first, second)), (os_ref, jnp.where(even, second, first))):
                left, right = part[:, :lanes], part[:, lanes:]
                ref[0, target] = jnp.where(side == 0, left, right).astype(BF16)
                ref[1, target] = jnp.where(side == 0, right, left).astype(BF16)

    if number == 1:

        @pl.when(chunk == pl.num_programs(0) - 1)
        def finish():
            grad, gain_part, shift_part = norm_backward(
                after_cross_ref[...], gain_ref[2:3], gnf[...]
            )
            grad = gc_ref[...] + grad
            gc_ref[...] = grad
            low = grad.astype(BF16)
            gco_ref[...] = low
            gcm_ref[...] = dot(low, co_ref[...], NT).astype(BF16)
            vec_ref[4:5] = gain_part
            vec_ref[5:6] = shift_part
            vec_ref[6:7] = row_sums(low)


def experts_backward(
    number, scalars, grad_final, after_ffn, act, slope, w_in, w_out, ordered, gain, parts, carried,
    after_cross=None, cross_out=None, before=(),
):
    unused, tokens, hidden = act.shape
    width = ordered.shape[1]
    block = hidden // FF_CHUNKS
    size = hidden // parts
    plain = size % LANES != 0
    fixed = lambda shape: pl.BlockSpec(shape, lambda c, scalars: (0,) * len(shape))
    out = lambda shape, dtype: jax.ShapeDtypeStruct(shape, dtype)
    bias_spec = pl.BlockSpec((EXPERT_ROWS, block), lambda c, scalars: (0, c))
    extra = list(carried) + ([after_cross, cross_out] if number == 1 else [])
    if plain:
        out_terms = [
            (
                pl.BlockSpec((2, block, width // 2), lambda c, scalars: (0, c, 0)),
                out((2, hidden, width // 2), BF16),
            ),
            (fixed((8, LANES)), out((8, LANES), BF16)),
        ]
    else:
        shape = (2, parts // 2, size, width // 2)
        out_terms = [(fixed(shape), out(shape, BF16))] * 2
    in_term = (
        pl.BlockSpec((1, 2, width // 2, block // 2), lambda c, scalars: (c, 0, 0, 0)),
        out((FF_CHUNKS, 2, width // 2, block // 2), BF16),
    )
    square = (tokens, width)
    outs = [in_term, in_term] + out_terms + [
        (bias_spec, out((EXPERT_ROWS, hidden), F32)),
        (fixed((8 + EXPERT_ROWS, width)), out((8 + EXPERT_ROWS, width), F32)),
        (fixed(square), out(square, F32)),
    ]
    scratch = [pltpu.VMEM(square, BF16)]
    if number == 1:
        outs += [(fixed(square), out(square, BF16))] * 2
        scratch.append(pltpu.VMEM(square, F32))
    else:
        outs.append((fixed(square), out(square, F32)))
    return pl.pallas_call(
        without(
            lambda *refs: experts_backward_kernel(number, plain, *refs), 9 + len(extra), len(before)
        ),
        grid_spec=pltpu.PrefetchScalarGridSpec(
            num_scalar_prefetch=1,
            grid=(FF_CHUNKS,),
            in_specs=[
                pl.BlockSpec(square, lambda c, scalars: (number, 0)),
                pl.BlockSpec((1,) + square, lambda c, scalars: (number, 0, 0)),
                pl.BlockSpec((1, tokens, block), lambda c, scalars: (number, 0, c)),
                pl.BlockSpec((1, tokens, block), lambda c, scalars: (number, 0, c)),
                pl.BlockSpec((1, width, block), lambda c, scalars: (scalars[0], 0, c)),
                pl.BlockSpec((1, block, width), lambda c, scalars: (scalars[0], c, 0)),
                fixed((tokens, width)),
                fixed((4, width)),
            ]
            + [bias_spec if place == 0 else fixed(array.shape) for place, array in enumerate(extra)]
            + [ANY] * len(before),
            out_specs=[spec for spec, unused in outs],
            scratch_shapes=scratch,
        ),
        out_shape=[shape for unused, shape in outs],
        compiler_params=kernel_params(48),
        cost_estimate=kernel_cost(4 * tokens * width * hidden, 2**24, 0),
    )(scalars, grad_final, after_ffn, act, slope, w_in, w_out, ordered, gain, *extra, *before)


def merge_slots_kernel(
    names_ref, i0, i1, i2, i3, o0, o1, o2, o3, in_keep, in_leave, out_keep, out_leave
):
    step = pl.program_id(0)
    experts = in_keep.shape[0]

    def merged(slots, expert):
        total = 0.0
        for number, slot in enumerate(slots):
            value = slot[...].astype(F32)
            total = total + jnp.where(names_ref[number] == expert, value, 0.0)
        return total.astype(BF16)

    def store(in_ref, out_ref):
        for expert in range(experts):
            in_ref[expert] = merged((i0, i1, i2, i3), expert)
            out_ref[expert] = merged((o0, o1, o2, o3), expert)

    pl.when(lax.rem(step, 2) == 0)(lambda: store(in_keep, out_keep))
    pl.when(lax.rem(step, 2) == 1)(lambda: store(in_leave, out_leave))


def merge_slots(names, in_slots, out_slots, experts):
    chunks, unused, places, rows_in, columns = in_slots[0].shape
    rows_out = out_slots[0].shape[2]
    place = lambda i: (i // 4) * 4 + lax.rem(i, 2) * 2 + lax.rem(i // 2, 2)
    in_block = (chunks, 2, 1, rows_in, columns)
    out_block = (2, 1, rows_out, columns)
    out = lambda shape: jax.ShapeDtypeStruct(shape, BF16)
    half = places // 2
    return pl.pallas_call(
        merge_slots_kernel,
        grid_spec=pltpu.PrefetchScalarGridSpec(
            num_scalar_prefetch=1,
            grid=(places,),
            in_specs=[pl.BlockSpec(in_block, lambda i, names: (0, 0, i, 0, 0))] * 4
            + [pl.BlockSpec(out_block, lambda i, names: (0, place(i), 0, 0))] * 4,
            out_specs=[
                pl.BlockSpec((experts,) + in_block, lambda i, names: (0, 0, 0, i // 2, 0, 0))
            ] * 2
            + [pl.BlockSpec((experts,) + out_block, lambda i, names: (0, 0, i // 2, 0, 0))] * 2,
        ),
        out_shape=[out((experts, chunks, 2, half, rows_in, columns))] * 2
        + [out((experts, 2, half, rows_out, columns))] * 2,
        compiler_params=kernel_params(40),
    )(names, *in_slots, *out_slots)


def cross_backward_kernel(
    side_ref, queries_ref, kv_ref, gcm_ref, seg_ref, mseg_ref, lse_ref, gc_ref, gco_ref, after_ref,
    gain_ref, cq_ref, so_ref, cross_mix_ref, nc_ref, self_mix_ref, order_ref, mem_ref, ckv_ref,
    memory_ref, gas_ref, gsm_ref, keep_ref, send_ref, vec_ref, dq, dkv,
):
    side = side_ref[0]
    half, width = gas_ref.shape
    cross_spans = span_lists(half, mem_ref.shape[0])[1]
    seg_query = seg_ref[:, pl.ds(pl.multiple_of(side * half, SPAN), half)].astype(F32)
    attend_backward(
        queries_ref, kv_ref, kv_ref, (0, 0, width), 0, gcm_ref, seg_query, as_column(mseg_ref[...]),
        lse_ref, cross_spans, False, dq, dkv.at[:, :width], dkv.at[:, width:],
    )
    grad, gain_part, shift_part = norm_backward(
        after_ref[...], gain_ref[1:2], dot(dq[...], cq_ref[...], NT)
    )
    grad = gc_ref[...] + grad
    gas_ref[...] = grad
    low = grad.astype(BF16)
    gsm_ref[...] = dot(low, so_ref[...], NT).astype(BF16)
    staged_terms(keep_ref, send_ref, 0, self_mix_ref[...], low, order_ref, side)
    staged_terms(keep_ref, send_ref, 1, cross_mix_ref[...], gco_ref[...], order_ref, side)
    staged_terms(keep_ref, send_ref, 2, nc_ref[...], dq[...], order_ref, side)
    grad_kv = dkv[...].astype(BF16)
    memory_ref[...] = dot(grad_kv, ckv_ref[...], NT).astype(BF16)
    for number in range(2):
        part = grad_kv[:, number * width : (number + 1) * width]
        staged_terms(keep_ref, send_ref, 3 + number, mem_ref[...], part, order_ref, side)
    vec_ref[...] = jnp.concatenate(
        [gain_part, shift_part, row_sums(low), row_sums(dq[...]), row_sums(grad_kv[:, width:])]
        + [jnp.zeros((3, width), F32)],
        axis=0,
    )


def cross_backward(side, *arrays):
    after, memory = arrays[8], arrays[16]
    half, width = after.shape
    mem_length = memory.shape[0]
    out = lambda shape, dtype: jax.ShapeDtypeStruct(shape, dtype)
    return pl.pallas_call(
        cross_backward_kernel,
        in_specs=[SMEM] + [VMEM] * 18,
        out_specs=[VMEM] * 6,
        out_shape=[
            out((mem_length, width), BF16),
            out((half, width), F32),
            out((half, width), BF16),
            out((5, 2, width // 2, width // 2), BF16),
            out((5, 2, width // 2, width // 2), BF16),
            out((8, width), F32),
        ],
        scratch_shapes=[
            pltpu.VMEM((half, width), BF16),
            pltpu.VMEM((mem_length, 2 * width), F32),
        ],
        compiler_params=kernel_params(56),
        cost_estimate=kernel_cost(24 * half * mem_length * width, 2**24, half * mem_length * 8),
    )(side, *arrays)


def self_backward_kernel(
    side_ref, qkv_ref, gsm_ref, seg_ref, lse_ref, dq_ref, halo_ref, own_ref, dkv
):
    side = side_ref[0]
    half, width = dq_ref.shape
    self_spans = span_lists(half, half)[0]
    seg_query, seg_key = self_segments(side, seg_ref, half)
    attend_backward(
        qkv_ref, qkv_ref, qkv_ref, (0, width, 2 * width), SPAN, gsm_ref, seg_query, seg_key, lse_ref,
        self_spans, True, dq_ref, dkv.at[:, :width], dkv.at[:, width:],
    )
    halo_ref[...] = dkv[:SPAN, :].astype(BF16)
    own_ref[...] = dkv[SPAN:, :]


def self_backward(side, qkv, grad_mix, segment, lse):
    half, width = grad_mix.shape
    out = lambda shape, dtype: jax.ShapeDtypeStruct(shape, dtype)
    return pl.pallas_call(
        self_backward_kernel,
        in_specs=[SMEM] + [VMEM] * 4,
        out_specs=[VMEM] * 3,
        out_shape=[
            out((half, width), BF16),
            out((SPAN, 2 * width), BF16),
            out((half, 2 * width), F32),
        ],
        scratch_shapes=[pltpu.VMEM((half + SPAN, 2 * width), F32)],
        compiler_params=kernel_params(48),
        cost_estimate=kernel_cost(16 * half * 2 * SPAN * width, 2**23, half * 2 * SPAN * 8),
    )(side, qkv, grad_mix, segment, lse)


def layer_end_kernel(
    side_ref, x_ref, dq_ref, own_ref, reached_ref, ns_ref, order_ref, si_ref, gas_ref, gain_ref,
    vec_ffn_ref, vec_cross_ref, bias_ref, input_ref, keep_ref, send_ref,
):
    side = side_ref[0]
    half, width = gas_ref.shape
    late = half - SPAN
    grad_kv = jnp.concatenate(
        [own_ref[:late, :], own_ref[late:, :] + reached_ref[...].astype(F32)], axis=0
    ).astype(BF16)
    thirds = [dq_ref[...], grad_kv[:, :width], grad_kv[:, width:]]
    grad_normed = sum(
        dot(third, si_ref[:, number * width : (number + 1) * width], NT)
        for number, third in enumerate(thirds)
    )
    grad, gain_part, shift_part = norm_backward(
        own_half(x_ref, side, half, SPAN).astype(F32), gain_ref[0:1], grad_normed
    )
    input_ref[...] = (gas_ref[...] + grad).astype(BF16)
    for number, third in enumerate(thirds):
        staged_terms(keep_ref, send_ref, number, ns_ref[...], third, order_ref, side)
    ffn, cross = vec_ffn_ref, vec_cross_ref
    vectors = [
        gain_part, cross[0:1], ffn[4:5], ffn[0:1], shift_part, cross[1:2], ffn[5:6], ffn[1:2],
        row_sums(thirds[0]), row_sums(thirds[2]), cross[2:5], ffn[6:7], ffn[8:], bias_ref[...],
    ]
    vectors = jnp.concatenate(vectors, axis=0)
    lanes = keep_ref.shape[3]
    vectors = jnp.concatenate(
        [vectors, jnp.zeros((lanes - vectors.shape[0], width), F32)], axis=0
    ).astype(BF16)
    term = dot(order_ref[...], vectors, (((0,), (1,)), ((), ()))).astype(BF16)
    middle = width // 2
    for number in range(2):
        keep_ref[3, number] = term[:middle]
        send_ref[3, number] = term[middle:]


def layer_end(side, *arrays):
    grad_after_self = arrays[7]
    half, width = grad_after_self.shape
    out = lambda shape, dtype: jax.ShapeDtypeStruct(shape, dtype)
    return pl.pallas_call(
        layer_end_kernel,
        in_specs=[SMEM] + [VMEM] * 12,
        out_specs=[VMEM] * 3,
        out_shape=[
            out((half, width), BF16),
            out((4, 2, width // 2, width // 2), BF16),
            out((4, 2, width // 2, width // 2), BF16),
        ],
        compiler_params=kernel_params(48),
        cost_estimate=kernel_cost(7 * half * width * width, 2**23, 0),
    )(side, *arrays)


def word_rows(lse, gap, counted_ref, shift_ref, lift_ref, div_ref):
    tokens = counted_ref.shape[1]
    counted = counted_ref[...] > 0
    lse_0, lse_1 = lse[:, :tokens], lse[:, tokens:]
    apart = lse_0 - lse_1
    kl_0 = gap[:, :tokens] - apart
    kl_1 = apart - gap[:, tokens:]
    shift_ref[:, :tokens] = jnp.where(counted, lse_0 - math.log(KL_WEIGHT), 1e30)
    shift_ref[:, tokens:] = jnp.where(counted, lse_1 - math.log(KL_WEIGHT), 1e30)
    lift_ref[:, :tokens] = (1.0 + 1.0 / KL_WEIGHT) - kl_0 - apart
    lift_ref[:, tokens:] = (1.0 + 1.0 / KL_WEIGHT) - kl_1 + apart
    div_ref[...] = kl_0 + kl_1


WORD_ROWS = 256


def word_stats_kernel(
    e_ref, f_ref, counted_ref, target_ref, z_ref, lse_ref, shift_ref, lift_ref, div_ref, zsum_ref,
    pick_ref, fits_ref, ft, total, weighted, zsum, picked,
):
    step = pl.program_id(0)

    @pl.when(step == 0)
    def start():
        ft[...] = f_ref[...].T
        for ref in (total, weighted, zsum, picked):
            ref[...] = jnp.zeros_like(ref)

    words = e_ref.shape[1]
    tokens = counted_ref.shape[1]
    fold = lambda values: jnp.sum(values.reshape(values.shape[0] // 8, 8, LANES), axis=0)
    units = [
        (block, low, min(low + WORD_ROWS, words))
        for block in range(tokens // LANES)
        for low in range(0, words, WORD_ROWS)
    ]

    def product(unit):
        block, low, high = unit
        first = slice(LANES * block, LANES * (block + 1))
        second = slice(tokens + LANES * block, tokens + LANES * (block + 1))
        return dot(e_ref[0, low:high, :], jnp.concatenate([ft[:, first], ft[:, second]], axis=1))

    coming = product(units[0])
    for number, (block, low, high) in enumerate(units):
        first = slice(LANES * block, LANES * (block + 1))
        second = slice(tokens + LANES * block, tokens + LANES * (block + 1))
        logits = coming
        coming = product(units[number + 1]) if number + 1 < len(units) else None
        left, right = logits[:, :LANES], logits[:, LANES:]
        z_ref[0, low:high, first] = left
        z_ref[0, low:high, second] = right
        apart = left - right
        word_ids = lax.broadcasted_iota(jnp.int32, (high - low, LANES), 0)
        hit = word_ids == (target_ref[:, first] - (step * words + low))
        for cols, values in ((first, left), (second, right)):
            exponent = jnp.exp(values)
            total[:, cols] += fold(exponent)
            weighted[:, cols] += fold(exponent * apart)
            zsum[:, cols] += fold(values)
            picked[:, cols] += fold(jnp.where(hit, values, 0.0))

    @pl.when(step == pl.num_programs(0) - 1)
    def finish():
        column_sum = lambda ref: jnp.sum(ref[...], axis=0, keepdims=True)
        whole = column_sum(total)
        gap = column_sum(weighted)
        inside = (whole > 1e-20) & (whole < 1e30) & (jnp.abs(gap) < 1e30)
        fits_ref[0, 0] = jnp.min(jnp.where(inside, 1.0, 0.0))
        lse = jnp.log(whole)
        lse_ref[...] = lse
        word_rows(lse, gap / whole, counted_ref, shift_ref, lift_ref, div_ref)
        zsum_ref[...] = column_sum(zsum)
        pick_ref[...] = column_sum(picked)


def word_stats(parts, final, counted, target):
    count, words, width = parts.shape
    columns = final.shape[0]
    fixed = lambda shape: pl.BlockSpec(shape, lambda i: (0, 0))
    shape = lambda dims: jax.ShapeDtypeStruct(dims, F32)
    row, half_row = (1, columns), (1, columns // 2)
    return pl.pallas_call(
        word_stats_kernel,
        grid=(count,),
        in_specs=[
            pl.BlockSpec((1, words, width), lambda i: (i, 0, 0)),
            fixed((columns, width)),
            fixed(half_row),
            fixed(half_row),
        ],
        out_specs=[pl.BlockSpec((1, words, columns), lambda i: (i, 0, 0))]
        + [fixed(row)] * 3
        + [fixed(half_row)]
        + [fixed(row)] * 2
        + [SMEM],
        out_shape=[shape((count, words, columns))]
        + [shape(row)] * 3
        + [shape(half_row)]
        + [shape(row)] * 2
        + [shape((1, 1))],
        scratch_shapes=[pltpu.VMEM((width, columns), BF16)] + [pltpu.VMEM((8, columns), F32)] * 4,
        compiler_params=kernel_params(48),
        cost_estimate=kernel_cost(
            count * words * width * columns, 5 * count * words * columns, count * words * columns
        ),
    )(parts, final, counted, target)


def shifted_stats_kernel(z_ref, counted_ref, lse_ref, shift_ref, lift_ref, div_ref, peak, total, weighted):
    step = pl.program_id(0)

    @pl.when(step == 0)
    def start():
        peak[...] = jnp.full_like(peak, -3e38)
        total[...] = jnp.zeros_like(total)
        weighted[...] = jnp.zeros_like(weighted)

    words = z_ref.shape[1]
    tokens = counted_ref.shape[1]
    for block in range(tokens // LANES):
        first = slice(LANES * block, LANES * (block + 1))
        second = slice(tokens + LANES * block, tokens + LANES * (block + 1))
        left = z_ref[0, :, first].reshape(words // 8, 8, LANES)
        right = z_ref[0, :, second].reshape(words // 8, 8, LANES)
        apart = left - right
        for cols, values in ((first, left), (second, right)):
            old_peak = peak[:, cols]
            new_peak = jnp.maximum(old_peak, jnp.max(values, axis=0))
            shrink = jnp.exp(old_peak - new_peak)
            exponent = jnp.exp(values - new_peak[None])
            peak[:, cols] = new_peak
            total[:, cols] = total[:, cols] * shrink + jnp.sum(exponent, axis=0)
            weighted[:, cols] = weighted[:, cols] * shrink + jnp.sum(exponent * apart, axis=0)

    @pl.when(step == pl.num_programs(0) - 1)
    def finish():
        top = jnp.max(peak[...], axis=0, keepdims=True)
        shrink = jnp.exp(peak[...] - top)
        whole = jnp.sum(total[...] * shrink, axis=0, keepdims=True)
        lse = top + jnp.log(whole)
        lse_ref[...] = lse
        gap = jnp.sum(weighted[...] * shrink, axis=0, keepdims=True) / whole
        word_rows(lse, gap, counted_ref, shift_ref, lift_ref, div_ref)


def shifted_stats(logits, counted):
    count, words, columns = logits.shape
    fixed = lambda shape: pl.BlockSpec(shape, lambda i: (0, 0))
    row, half_row = (1, columns), (1, columns // 2)
    return pl.pallas_call(
        shifted_stats_kernel,
        grid=(count,),
        in_specs=[pl.BlockSpec((1, words, columns), lambda i: (i, 0, 0)), fixed(half_row)],
        out_specs=[fixed(row)] * 3 + [fixed(half_row)],
        out_shape=[jax.ShapeDtypeStruct(row, F32)] * 3 + [jax.ShapeDtypeStruct(half_row, F32)],
        scratch_shapes=[pltpu.VMEM((8, columns), F32)] * 3,
        compiler_params=kernel_params(48),
    )(logits, counted)


def word_grads_kernel(
    place, first_part, begins, vocab, e_ref, z_ref, f_ref, shift_ref, lift_ref, base_ref, target_ref,
    *refs
):
    if vocab:
        lse_ref, div_ref, zsum_ref, pick_ref, *refs = refs
    if not begins:
        old_gft_ref, *refs = refs
    if vocab:
        keep_ref, send_ref, gf_ref, loss_ref, grads, gft_ref = refs
    else:
        keep_ref, send_ref, gft_ref, grads = refs
    step = pl.program_id(0)

    @pl.when(step == 0)
    def start():
        gft_ref[...] = jnp.zeros_like(gft_ref) if begins else old_gft_ref[...]

    words = e_ref.shape[1]
    tokens = target_ref.shape[1]
    first_word = (place[0] ^ (first_part + step)) * words
    word_ids = lax.broadcasted_iota(jnp.int32, (words, LANES), 0)
    for block in range(tokens // LANES):
        first = slice(LANES * block, LANES * (block + 1))
        second = slice(tokens + LANES * block, tokens + LANES * (block + 1))
        left = z_ref[0, :, first]
        right = z_ref[0, :, second]
        hit = word_ids == (target_ref[:, first] - first_word)
        plain = jnp.where(hit, base_ref[1:2, first], base_ref[0:1, first])
        prob_left = jnp.exp(left - shift_ref[:, first])
        prob_right = jnp.exp(right - shift_ref[:, second])
        apart = left - right
        grad_left = prob_left * (apart + lift_ref[:, first]) - prob_right + plain
        grad_right = prob_right * (lift_ref[:, second] - apart) - prob_left + plain
        grads[:, first] = grad_left.astype(BF16)
        grads[:, second] = grad_right.astype(BF16)
    term = dot(grads[...], f_ref[...]).astype(BF16)
    lanes = term.shape[1] // 2

    def store(ref):
        ref[0, 0] = term[:, :lanes]
        ref[0, 1] = term[:, lanes:]

    pl.when(lax.rem(step, 2) == 0)(lambda: store(keep_ref))
    pl.when(lax.rem(step, 2) == 1)(lambda: store(send_ref))
    gft_ref[...] += dot(e_ref[0], grads[...], TN)

    if vocab:

        @pl.when(step == pl.num_programs(0) - 1)
        def finish():
            gf_ref[...] = gft_ref[...].T
            lse = lse_ref[...]
            smoothed = -(1.0 - SMOOTHING) * (pick_ref[...] - lse) - SMOOTHING / vocab * (
                zsum_ref[...] - vocab * lse
            )
            halves = 0.5 * KL_WEIGHT * div_ref[...]
            counted = target_ref[...] >= 0
            loss_ref[:, :tokens] = jnp.where(counted, smoothed[:, :tokens] + halves, 0.0)
            loss_ref[:, tokens:] = jnp.where(counted, smoothed[:, tokens:] + halves, 0.0)


def word_grads(parts, place, first_part, count, logits, fixed_args, end_args, carried):
    total, words, width = parts.shape
    columns = logits.shape[2]
    vocab = total * words if end_args else 0
    fixed = lambda shape: pl.BlockSpec(shape, lambda i, place: (0,) * len(shape))
    picked = lambda shape: pl.BlockSpec(shape, lambda i, place: (place[0] ^ (first_part + i), 0, 0))
    extra = list(fixed_args) + list(end_args) + list(carried)
    ends = [(columns, width), (1, columns)] if vocab else [(width, columns)]
    scratch = [pltpu.VMEM((words, columns), BF16)]
    if vocab:
        scratch.append(pltpu.VMEM((width, columns), F32))
    term = (2, words, width // 2)
    return pl.pallas_call(
        lambda place, *refs: word_grads_kernel(place, first_part, not carried, vocab, *refs),
        grid_spec=pltpu.PrefetchScalarGridSpec(
            num_scalar_prefetch=1,
            grid=(count,),
            in_specs=[picked((1, words, width)), picked((1, words, columns))]
            + [fixed(array.shape) for array in extra],
            out_specs=[pl.BlockSpec((1,) + term, lambda i, place: (i // 2, 0, 0, 0))] * 2
            + [fixed(shape) for shape in ends],
            scratch_shapes=scratch,
        ),
        out_shape=[jax.ShapeDtypeStruct((count // 2,) + term, BF16)] * 2
        + [jax.ShapeDtypeStruct(shape, F32) for shape in ends],
        compiler_params=kernel_params(48),
        cost_estimate=kernel_cost(
            3 * count * words * width * columns, 8 * count * words * width, count * words * columns
        ),
    )(place, parts, logits, *extra)


def first_zero(array):
    if isinstance(array, tuple):
        return sum(first_zero(one) for one in array)
    return lax.slice(array, (0,) * array.ndim, (1,) * array.ndim).reshape(()).astype(F32) * 0.0


def tie(first, second):
    return lax.optimization_barrier((first, second))


class Places:
    def __init__(self):
        self.row = lax.axis_index("rows")
        self.side = lax.axis_index("pass")
        self.rows = lax.axis_size("rows")
        self.bits = self.rows.bit_length() - 1

    def send(self, array, stage):
        if stage == "pass":
            return lax.ppermute(array, "pass", [(0, 1), (1, 0)])
        flip = 1 << stage
        return lax.ppermute(array, "rows", [(i, i ^ flip) for i in range(self.rows)])

    def in_order(self, own, other, axis):
        first = jnp.where(self.side == 0, own, other)
        second = jnp.where(self.side == 0, other, own)
        return jnp.concatenate([first, second], axis=axis)

    def pass_columns(self, array):
        half = array.shape[-1] // 2
        first, second = array[..., :half], array[..., half:]
        return jnp.concatenate(
            [jnp.where(self.side == 0, first, second), jnp.where(self.side == 0, second, first)],
            axis=-1,
        )

    def row_order(self, width):
        size = width // self.rows
        k = jnp.arange(width, dtype=jnp.int32)
        rest = k // size
        j = (rest % (self.rows // 2)) * 2 + rest // (self.rows // 2)
        source = (self.row ^ j) * size + k % size
        return (jnp.arange(width, dtype=jnp.int32)[:, None] == source[None, :]).astype(BF16)


class Stream:
    def __init__(self, places, axes, lead, dense, stages, experts=0):
        self.places = places
        self.axis = {stage: lead + number for number, stage in enumerate(axes)}
        self.dense = list(dense)
        self.slots = []
        self.stages = list(stages)
        self.experts = experts
        self.waiting = []
        self.flight = []

    def cut(self, stage, index):
        def take(array, lead):
            return lax.slice_in_dim(array, index, index + 1, 1, self.axis[stage] + lead)

        lead = 1 if self.experts else 0
        return (
            [take(array, lead) for array in self.dense],
            [(take(array, 0), name) for array, name in self.slots],
        )

    def total(self, dense=None, slots=None, pin=None):
        if dense is None:
            dense, slots = self.dense, self.slots
        result = 0.0 if pin is None else first_zero(pin)
        if slots:
            ids = jnp.arange(self.experts, dtype=jnp.int32).reshape((-1,) + (1,) * slots[0][0].ndim)
            for array, name in slots:
                result = result + jnp.where(ids == name, array[None], jnp.zeros((), BF16)).astype(F32)
        for array in dense:
            result = result + array.astype(F32)
        return result.astype(BF16)

    def launch(self, array, stage, name=None):
        self.flight.append((self.places.send(array, stage), name))

    def take(self, arrays):
        for array, (unused, name) in zip(arrays, self.flight):
            if name is None:
                self.dense.append(array)
            else:
                self.slots.append((array, name))
        self.flight = []

    def leave(self, pin=None):
        stage = self.stages.pop(0)
        self.waiting = [(self.total(*self.cut(stage, 1), pin), stage)]
        dense, slots = self.cut(stage, 0)
        self.dense = [self.total(dense, slots)] if slots else dense
        self.slots = []

    def go(self, arrays):
        for array, (unused, stage) in zip(arrays, self.waiting):
            self.launch(array, stage)
            self.sent = array
        self.waiting = []

    def share(self, pin=None):
        self.own = self.total(pin=pin)
        self.waiting = [(self.own, "pass")]
        self.dense = []

    def finished(self, pin=None):
        other = self.dense[0] if self.dense else self.flight[0][0]
        if pin is not None:
            other = other + first_zero(pin).astype(BF16)
        return self.places.in_order(self.own, other, -1).astype(F32)


class Gather:
    def __init__(self, places, stage, sources, targets, share=False):
        self.places, self.stage, self.sources, self.targets = places, stage, sources, targets
        self.flight = []

    def leave(self, pin=None):
        totals = [source.total(pin=pin) for source in self.sources]
        self.waiting = [(jnp.concatenate(totals, axis=0), None)]

    def go(self, arrays):
        self.flight = [(self.places.send(arrays[0], self.stage), None)]

    def take(self, arrays):
        step = arrays[0].shape[0] // len(self.targets)
        for number, target in enumerate(self.targets):
            target.dense.append(arrays[0][number * step : (number + 1) * step])


def settle(values, landing=(), leaving=(), pin=None):
    arrays = [[array for array, unused in stream.flight] for stream in landing]
    values, arrays = tie(values, arrays)
    for stream, landed in zip(landing, arrays):
        stream.take(landed)
    if leaving:
        for stream in leaving:
            stream.leave(pin)
        arrays = [[entry[0] for entry in stream.waiting] for stream in leaving]
        values, arrays = tie(values, arrays)
        for stream, going in zip(leaving, arrays):
            stream.go(going)
    return values


def on_device(
    layer_in, memory, targets, segment_ids, memory_segments, row_length, group_sizes, pass_experts,
    norm_gain, norm_bias, self_in, self_out, cross_query, cross_key_value, cross_out,
    attention_bias, expert_in, expert_in_bias, expert_out, expert_out_bias, embedding,
):
    length = segment_ids.shape[1]
    mem_length = memory_segments.shape[1]
    width = layer_in.shape[1]
    half = length // 2
    mem_half = mem_length // 2
    vocab = embedding.shape[0]
    hidden = expert_in.shape[2]
    expert_count = expert_in.shape[0]
    side = lax.axis_index("pass")
    places = Places()
    rows, bits = places.rows, places.bits
    place = places.row.reshape(1)
    side_word = side.reshape(1)
    start = side * half

    other_experts = places.send(pass_experts, "pass")
    names, *scalars = expert_names(group_sizes, pass_experts, other_experts, place, side_word)
    experts, sibling = names[:2], names[2:]
    row_order = places.row_order(width)
    own_target = lax.dynamic_slice_in_dim(targets, start, half, 0)
    counted = start + jnp.arange(half, dtype=jnp.int32) < row_length[0]

    (normed_self, qkv, self_mix, self_lse, after_self, normed_cross, cross_queries, memory_kv,
     cross_mix, cross_lse, after_cross, normed_ffn) = layer_forward(
        side_word, layer_in, memory, segment_ids, memory_segments, norm_gain, norm_bias,
        (self_in, self_out, cross_query, cross_key_value, cross_out), attention_bias,
    )
    activation, slope, final, after_ffn = experts_forward(
        names, normed_ffn, after_cross, expert_in, expert_in_bias, expert_out, expert_out_bias,
        norm_gain, norm_bias,
    )
    ffn_order = dot(normed_ffn, row_order).astype(BF16)
    base_all = jnp.where(counted, -SMOOTHING / vocab, 0.0)
    base = jnp.stack([base_all, base_all - (1.0 - SMOOTHING)])
    target_row = jnp.where(counted, own_target, -1).reshape(1, half)
    counted_row = counted.astype(F32).reshape(1, half)
    final_halves = places.pass_columns(final)
    (final, final_halves, row_order, ffn_order, base, target_row, counted_row) = (
        lax.optimization_barrier(
            (final, final_halves, row_order, ffn_order, base, target_row, counted_row)
        )
    )

    size = vocab // rows
    fine = size % 8 == 0 and bits == 4
    block = size if fine else (800 if vocab % 1600 == 0 else vocab // 2)
    parts = embedding.reshape(-1, block, width)
    logits, *stats, zsum, picks, fits = word_stats(parts, final, counted_row, target_row)
    lse, shift, lift, divergence = lax.cond(
        fits[0, 0] > 0.5, lambda: tuple(stats), lambda: tuple(shifted_stats(logits, counted_row))
    )
    word_args = (final_halves, shift, lift, base, target_row)
    end_args = (lse, divergence, zsum, picks)
    emb = {}
    if fine:
        quarter = rows // 4
        carried = []
        moves = {1: ((), ()), 3: ((1,), (1,)), 0: ((1, 3), (3, 1)), 2: ((3, 1, 0), (0, 3))}
        for number, high in enumerate(moves):
            keep, send, *carried = word_grads(
                parts, place, high * quarter, quarter, logits, word_args,
                end_args if number == 3 else (), tuple(carried),
            )
            landing, leaving = moves[high]
            keep, send, carried = settle(
                (keep, send, carried), [emb[k] for k in landing], [emb[k] for k in leaving]
            )
            emb[high] = Stream(places, [1, "pass"], 0, [keep], [1, "pass"])
            emb[high].launch(send, 0)
    else:
        keep, send, *carried = word_grads(
            parts, jnp.zeros_like(place), 0, vocab // block, logits, word_args, end_args, ()
        )
        natural = jnp.moveaxis(jnp.stack([keep, send], axis=1), 2, 0).reshape(2, rows, size, width // 2)
        ordered = natural[:, places.row ^ jnp.arange(rows)]
        ordered = ordered.reshape((2,) * (bits + 1) + (size, width // 2))
        emb[0] = Stream(
            places, ["pass"] + list(range(bits - 1, -1, -1)), 0, [ordered],
            list(range(bits)) + ["pass"],
        )
    grad_final, losses = carried
    loss_0, loss_1 = losses[0, :half], losses[0, half:]
    mine = jnp.where(side == 0, loss_0, loss_1)
    partners = places.send(jnp.where(side == 0, loss_1, loss_0), "pass")
    token_loss = places.in_order(mine, partners, 0).reshape(1, -1)

    high_first = list(range(bits - 1, 0, -1))
    others = list(range(2, bits))
    axes = ["pass"] + high_first
    in_stream = Stream(places, axes, 1, [], [1, 2, "pass"] + others[1:], expert_count)
    out_stream = Stream(places, axes, 0, [], [2, 1, "pass"] + others[1:], expert_count)
    in_shape = (FF_CHUNKS,) + (2,) * bits + (width // rows, hidden // (2 * FF_CHUNKS))
    out_shape = (2,) * bits + (hidden // rows, width // 2)
    carried = ()
    before = [emb[0].sent, emb[3].sent] if fine else []
    for number in range(2):
        ends = {} if number == 0 else {"after_cross": after_cross, "cross_out": cross_out}
        made = experts_backward(
            number, scalars[number], grad_final, after_ffn, activation, slope, expert_in, expert_out,
            ffn_order, norm_gain, rows, carried, before=before, **ends,
        )
        if fine:
            if number == 0:
                made = settle(made, [emb[3], emb[2]], [emb[2]])
                before = [emb[2].sent]
            else:
                made = settle(made, [emb[0], in_stream, out_stream], [emb[0]])
        in_keep, in_send, out_keep, out_send, bias_term, vec_ffn, grad_after_cross, *carried = made
        if out_keep.ndim == 3:
            natural = out_keep.reshape(2, rows, hidden // rows, width // 2)
            natural = natural[:, places.row ^ jnp.arange(rows)]
            out_keep, out_send = natural[:, 0::2], natural[:, 1::2]
        in_stream.slots.append((in_keep.reshape(in_shape), experts[number]))
        in_stream.launch(in_send.reshape(in_shape), 0, sibling[number])
        out_stream.slots.append((out_keep.reshape(out_shape), experts[number]))
        out_stream.launch(out_send.reshape(out_shape), 0, sibling[number])
        if number == 0:
            carried = (bias_term, grad_after_cross, carried[0], vec_ffn)
    grad_cross_out, grad_cross_mix = carried

    if fine:
        grad_cross_mix = settle(grad_cross_mix, [in_stream, out_stream], [])
        flat = lambda array, lead: array.reshape(array.shape[:lead] + (rows // 2,) + array.shape[-2:])
        in_keep, in_leave, out_keep, out_leave = merge_slots(
            names,
            [flat(in_stream.slots[number][0], 2) for number in (0, 2, 1, 3)],
            [flat(out_stream.slots[number][0], 1) for number in (0, 2, 1, 3)],
            expert_count,
        )
        in_tail, out_tail = in_keep.shape[-2:], out_keep.shape[-2:]
        in_shape = (expert_count, FF_CHUNKS, 2, 2, 2, 1) + in_tail
        out_shape = (expert_count, 2, 2, 1, 2) + out_tail
        (in_leave, out_leave), grad_cross_mix = tie((in_leave, out_leave), grad_cross_mix)
        for stream, keep, leave, shape in (
            (in_stream, in_keep, in_leave, in_shape),
            (out_stream, out_keep, out_leave, out_shape),
        ):
            stream.slots = []
            stream.dense = [keep.reshape(shape)]
            stream.launch(leave.reshape(shape), stream.stages.pop(0))
    made = cross_backward(
        side_word, cross_queries, memory_kv, grad_cross_mix, segment_ids,
        memory_segments, cross_lse, grad_after_cross, grad_cross_out, after_self, norm_gain,
        cross_query, self_out, cross_mix, normed_cross, self_mix, row_order, memory, cross_key_value,
    )
    if fine:
        emb_z0 = Gather(places, 2, [emb[1], emb[3]], [emb[0], emb[2]])
        made = settle(made, [emb[2], emb[0]], [emb[2], emb_z0])
    memory_part, grad_after_self, grad_self_mix, mid_keep, mid_send, vec_cross = made
    block_shape = (-1,) + (2,) * bits + (width // rows, width // 2)
    small_stages = [1, "pass"] + others
    mid_stream = Stream(places, axes, 1, [mid_keep.reshape(block_shape)], small_stages)
    mid_stream.launch(mid_send.reshape(block_shape), 0)
    memory_other = places.send(memory_part, "pass")
    made = self_backward(side_word, qkv, grad_self_mix, segment_ids, self_lse)
    made = lax.optimization_barrier(made)
    grad_sq, halo_kv, own_kv = made
    reached = lax.ppermute(halo_kv, "pass", [(1, 0)])
    part = width // rows
    bias_rows = bias_term[:expert_count].reshape(expert_count, rows, -1, part)
    bias_rows = jnp.moveaxis(bias_rows, 1, 2).reshape(-1, width)
    if fine:
        grad_sq = settle(grad_sq, [in_stream, out_stream], [in_stream, out_stream], halo_kv)
        grad_sq = settle(grad_sq, [mid_stream], [mid_stream], in_stream.sent)
    reached, grad_sq, bias_rows = lax.optimization_barrier((reached, grad_sq, bias_rows))
    made = layer_end(
        side_word, layer_in, grad_sq, own_kv, reached, normed_self, row_order, self_in,
        grad_after_self, norm_gain, vec_ffn, vec_cross, bias_rows,
    )
    made = lax.optimization_barrier(made)
    if fine:
        emb_z1 = Gather(places, 3, [emb[2]], [emb[0]])
        made = settle(made, [emb[2], emb_z0], [emb_z1], made[2])
    input_own, late_keep, late_send = made
    late_stream = Stream(places, axes, 1, [late_keep.reshape(block_shape)], small_stages)
    late_stream.launch(late_send.reshape(block_shape), 0)
    token = jnp.zeros((8, LANES), F32)
    if fine:
        token = settle(
            token, [in_stream, out_stream], [in_stream, out_stream], (late_send, memory_other)
        )
        token = settle(token, [late_stream], [late_stream], out_stream.sent)
        input_other = places.send(input_own, "pass")
        token = settle(token, [emb_z1], [])
        emb[0].share(late_stream.sent)
        token, emb[0].own = tie(token, emb[0].own)
        emb[0].go([emb[0].own])
        token = settle(token, [in_stream, out_stream], [in_stream, out_stream], emb[0].own)
        token = settle(token, [late_stream, mid_stream], [])
        both = Stream(places, axes, 1, [], others)
        joined = []
        for index in (1, 0):
            pieces = [
                stream.total(*stream.cut("pass", index), out_stream.sent)
                for stream in (mid_stream, late_stream)
            ]
            joined.append(jnp.concatenate(pieces, axis=0))
        joined, token = tie(joined, token)
        both.dense = [joined[1]]
        both.launch(joined[0], "pass")
        token = settle(token, [both], [both], joined[0])
        token = settle(token, [in_stream, out_stream], [])
        in_stream.share(both.sent)
        out_stream.share(both.sent)
        shared, token = tie([in_stream.own, out_stream.own], token)
        in_stream.own, out_stream.own = shared
        in_stream.go([shared[0]])
        out_stream.go([shared[1]])
        token = settle(token, [both], [both], shared[1])
        token = settle(token, [both], [])
        both.share(both.sent)
        both.go([both.own])
    else:
        input_other = places.send(input_own, "pass")
        for stream in (emb[0], in_stream, out_stream, mid_stream, late_stream):
            while stream.stages:
                token = settle(token, [stream], [stream])
            token = settle(token, [stream], [])
            stream.share()
            stream.go([stream.own])
    reduced_embedding = emb[0].finished(shared[1] if fine else None).reshape(size, width)
    reduced_in = in_stream.finished().reshape(expert_count, FF_CHUNKS, width // rows, -1)
    reduced_in = jnp.moveaxis(reduced_in, 1, 2).reshape(expert_count, width // rows, hidden)
    reduced_out = out_stream.finished().reshape(expert_count, hidden // rows, width)
    if fine:
        reduced = both.finished().reshape(9, width // rows, width)
        reduced_mid, reduced_late = reduced[:5], reduced[5:8]
        vectors = both.own[8]
    else:
        reduced_late = late_stream.finished().reshape(4, width // rows, width)[:3]
        reduced_mid = mid_stream.finished().reshape(5, width // rows, width)
        vectors = late_stream.own[3]
    side_by_side = lambda blocks: jnp.moveaxis(blocks, 0, 1).reshape(width // rows, -1)
    memory_other = memory_other.astype(F32)
    if fine:
        memory_other = memory_other + first_zero(both.own)
        input_other = input_other + first_zero(shared[1]).astype(BF16)
    memory_grad = memory_part.astype(F32) + memory_other
    input_grad = places.in_order(input_own, input_other, 0).astype(F32)
    vectors = vectors.reshape(part, -1).astype(F32).T
    g_gain, g_bias, g_attention_bias = vectors[0:4], vectors[4:8], vectors[8:14]
    g_expert_out_bias = vectors[14 : 14 + expert_count]
    low = 14 + EXPERT_ROWS
    g_expert_in_bias = vectors[low : low + expert_count * (hidden // width)].reshape(expert_count, -1)
    return (
        token_loss,
        input_grad,
        memory_grad,
        g_gain,
        g_bias,
        side_by_side(reduced_late),
        reduced_mid[0],
        reduced_mid[2],
        side_by_side(reduced_mid[3:]),
        reduced_mid[1],
        g_attention_bias,
        reduced_in,
        g_expert_in_bias,
        reduced_out,
        g_expert_out_bias,
        reduced_embedding,
    )


def solution(mesh):
    rows = P("rows", None)
    return jax.shard_map(
        on_device,
        mesh=mesh,
        in_specs=(rows, rows, P("rows"), rows, rows, P("rows"), P(), P("pass", None)) + (P(),) * 13,
        out_specs=(
            P("pass", "rows"), rows, rows, P(None, "rows"), P(None, "rows"), rows, rows, rows, rows,
            rows, P(None, "rows"), P(None, "rows", None), P(None, "rows"), P(None, "rows", None),
            P(None, "rows"), rows,
        ),
        check_vma=False,
    )
```
